512 devices in a mesh: row: 16 (over y, core), col: 32 (over x, z).
Axes of the slice: x: 4, y: 8, z: 8, core: 2. Of those that a mesh axis runs over, the one named last changes fastest.
Arguments:
- band_values: bfloat16 [2048, 64, 1536], P(('row', 'col')), may hold values from -0.3125 to 0.3125
- pattern: int32 [2048, 24], P(('row', 'col')), may hold values 0 or 1
Outputs:
- stepped: bfloat16 [2048, 64, 1536], P(('row', 'col'))
The draws below stay inside these ranges and needn't reach their ends.
All inputs are finite; a program needn't handle non-finite values. No bound on the sum of `pattern` on one device may be relied on, other than what follows from the above.
Results may differ from the reference program's by a relative error of at most 0.0033.
Values may be sent and summed in bfloat16 or wider, within the bound.
No kernel may reach another device: no remote copies, remote signals or barrier semaphores. Data moves between devices by JAX's collectives and lax.ppermute only.
A program may use at most 192 MiB of HBM per device.

```python
import jax
import jax.numpy as jnp

BLOCK = 64
NZ = 24
NB = 2048


def place_ends(entries, key, smallest, largest):
    place = [jax.random.randint(jax.random.fold_in(key, axis), (), 0, length) for axis, length in enumerate(entries.shape)]
    longest = entries.shape.index(max(entries.shape))
    beside = place[:longest] + [(place[longest] + 1) % entries.shape[longest]] + place[longest + 1:]
    return entries.at[tuple(place)].set(smallest).at[tuple(beside)].set(largest)


def block_levels(rng, shape, cuts, low, high):
    factor_of, own = 1.0, jax.random.fold_in(rng, 6)
    for position, parts in cuts:
        heights = jnp.exp(jax.random.uniform(jax.random.fold_in(own, position), (parts,), jnp.float32, low / len(cuts), high / len(cuts)))
        factor_of = factor_of * jnp.repeat(heights, shape[position] // parts).reshape([-1 if axis == position else 1 for axis in range(len(shape))])
    return factor_of


def noise(stream_key, shape, width, limit, cuts=(), held_as=jnp.bfloat16):
    level = block_levels(stream_key, shape, cuts, -0.22, 0.18) if cuts else 1.0
    values = jax.random.normal(stream_key, shape, jnp.float32) * width * level
    return jnp.minimum(jnp.maximum(values, -limit), limit).astype(held_as)


def setup_inputs(seed: int = 0) -> dict:
    seeds = jax.random.split(jax.random.key(seed), 3)
    return {
        "band_values": noise(seeds[0], (NB, BLOCK, NZ * BLOCK), (NZ * 16) ** -0.5, 0.3125, ((0, 512),)),
        "pattern": place_ends((jax.random.randint(seeds[1], (NB, NZ), 0, 4) < 3).astype(jnp.int32), jax.random.fold_in(seeds[1], 1), 0, 1),
    }


def band_product(left, source):
    half_band = NZ // 2
    row_count = left.shape[0]
    source_wide = source.astype(jnp.float32)
    totals = jnp.zeros((row_count, BLOCK, NZ, BLOCK), jnp.float32)
    for diag_index in range(NZ):
        left_block = left[:, :, diag_index * BLOCK:(diag_index + 1) * BLOCK].astype(jnp.float32)
        shifted = jnp.roll(source_wide, -(diag_index - half_band), axis=0)
        partial_value = jnp.einsum("rab,rbc->rac", left_block, shifted).reshape(row_count, BLOCK, NZ, BLOCK)
        lowest = max(0, diag_index - half_band)
        highest = min(NZ, NZ + diag_index - half_band)
        start = lowest - diag_index + half_band
        totals = totals.at[:, :, lowest:highest].add(partial_value[:, :, start:start + highest - lowest])
    return totals


def reference(band_values, pattern):
    keep = (pattern == 1)[:, None, :, None]
    shaped = band_values.reshape(NB, BLOCK, NZ, BLOCK)
    masked4 = jnp.where(keep, shaped, jnp.zeros_like(shaped))
    masked = masked4.reshape(NB, BLOCK, NZ * BLOCK)
    square = jnp.where(keep, band_product(masked, masked), 0.0).astype(jnp.bfloat16)
    square = square.reshape(NB, BLOCK, NZ * BLOCK)
    cubic = band_product(masked, square)
    result = jnp.where(keep, 1.5 * masked4.astype(jnp.float32) - 0.5 * cubic, 0.0)
    return result.astype(jnp.bfloat16).reshape(NB, BLOCK, NZ * BLOCK)
```

```python
import functools

import jax
import jax.numpy as jnp
from jax import lax
from jax.experimental import pallas as pl
from jax.experimental.pallas import tpu as pltpu
from jax.sharding import PartitionSpec as P

AXES = ("row", "col")
BLOCK = 64
ROWS = 4
TILE = ROWS * BLOCK
REACH = 3
TILES = 2 * REACH + 1
HEAD = 5 * BLOCK
BODY = 10 * TILE
TAIL = 3 * BLOCK
DATA = HEAD + BODY + TAIL
NOTE = 16
ALL = DATA + NOTE
F32 = jnp.float32
BF16 = jnp.bfloat16
VMEM = pl.BlockSpec(memory_space=pltpu.VMEM)
SMEM = pl.BlockSpec(memory_space=pltpu.SMEM)


def first_rows(tiles):
    return HEAD + (tiles - 1) * 2 * TILE


def last_rows(tiles):
    return TAIL + (tiles - 1) * 2 * TILE


def half_lanes(rows):
    return lax.broadcasted_iota(jnp.int32, (rows, 128), 1) < BLOCK


def swap_halves(piece):
    return pltpu.roll(piece.astype(F32), BLOCK, 1)


def pack_kernel(x_ref, pattern_ref, out_ref):
    low = half_lanes(BLOCK)
    zero = jnp.zeros((BLOCK, 128), F32)
    note = jnp.zeros((NOTE, 128), F32)
    lane = lax.broadcasted_iota(jnp.int32, (NOTE, 128), 1)
    row = lax.broadcasted_iota(jnp.int32, (NOTE, 128), 0)
    slots = x_ref.shape[2] // BLOCK
    strips = []
    for q in range(ROWS):
        pieces = []
        for pair in range(slots // 2):
            even = pattern_ref[q, 2 * pair]
            odd = pattern_ref[q, 2 * pair + 1]
            keep = jnp.where(low, even, odd) == 1
            piece = x_ref[q, :, pair * 128 : (pair + 1) * 128].astype(F32)
            pieces.append(jnp.where(keep, piece, 0.0))
            for slot, present in ((2 * pair, even), (2 * pair + 1, odd)):
                value = jnp.where(present == 1, 1.0, 0.0)
                note = jnp.where((row == q) & (lane == slot + q), value, note)
        shifted = [zero] * (q // 2)
        if q % 2 == 0:
            shifted += pieces
        else:
            turned = [swap_halves(piece) for piece in pieces]
            shifted.append(jnp.where(low, 0.0, turned[0]))
            for left, right in zip(turned[:-1], turned[1:]):
                shifted.append(jnp.where(low, left, right))
            shifted.append(jnp.where(low, turned[-1], 0.0))
        shifted += [zero] * (2 * TILES - len(shifted))
        strips.append(shifted)

    def put(start, piece):
        out_ref[start : start + BLOCK, :] = piece.astype(BF16)

    put(0, strips[0][0])
    put(BLOCK, strips[0][1])
    put(2 * BLOCK, strips[1][1])
    put(3 * BLOCK, strips[2][1])
    put(4 * BLOCK, jnp.where(low, swap_halves(strips[3][1]), strips[1][0]))
    for pair in range(2, 2 * TILES - 2):
        for q in range(ROWS):
            put(HEAD + (pair - 2) * TILE + q * BLOCK, strips[q][pair])
    put(HEAD + BODY, strips[2][2 * TILES - 2])
    put(HEAD + BODY + BLOCK, strips[3][2 * TILES - 2])
    put(
        HEAD + BODY + 2 * BLOCK,
        jnp.where(low, strips[1][2 * TILES - 2], swap_halves(strips[3][2 * TILES - 1])),
    )
    out_ref[DATA:, :] = note.astype(BF16)


def pack(x, pattern):
    return pl.pallas_call(
        pack_kernel,
        out_shape=jax.ShapeDtypeStruct((ALL, 128), BF16),
        in_specs=[VMEM, SMEM],
        out_specs=VMEM,
        compiler_params=pltpu.CompilerParams(vmem_limit_bytes=32 << 20),
        cost_estimate=pl.CostEstimate(flops=1 << 20, bytes_accessed=3 << 20, transcendentals=0),
    )(x, pattern)


def unpack_tile(source, tile, base, window, row, col):
    def put(q, half, piece):
        window[pl.ds(row + q * BLOCK, BLOCK), pl.ds(col + half * 128, 128)] = piece

    low = half_lanes(BLOCK)
    zero = jnp.zeros((BLOCK, 128), BF16)
    if tile == 0:

        def seg(k):
            return source[base + k * BLOCK : base + (k + 1) * BLOCK, :]

        mixed = seg(4)
        put(0, 0, seg(0))
        put(0, 1, seg(1))
        put(1, 0, jnp.where(low, 0.0, mixed.astype(F32)).astype(BF16))
        put(1, 1, seg(2))
        put(2, 0, zero)
        put(2, 1, seg(3))
        put(3, 0, zero)
        put(3, 1, jnp.where(low, 0.0, swap_halves(mixed)).astype(BF16))
    elif tile == TILES - 1:

        def seg(k):
            return source[base + k * BLOCK : base + (k + 1) * BLOCK, :]

        mixed = seg(2)
        put(0, 0, zero)
        put(0, 1, zero)
        put(1, 0, jnp.where(low, mixed.astype(F32), 0.0).astype(BF16))
        put(1, 1, zero)
        put(2, 0, seg(0))
        put(2, 1, zero)
        put(3, 0, seg(1))
        put(3, 1, jnp.where(low, swap_halves(mixed), 0.0).astype(BF16))
    else:
        for half in range(2):
            start = base + half * TILE
            window[row : row + TILE, col + half * 128 : col + half * 128 + 128] = source[start : start + TILE, :]


def tile_start(tile, first):
    def whole(t):
        return 0 if t == 0 else HEAD + (t - 1) * 2 * TILE

    return whole(tile) - whole(first)


def spread(note):
    lane = lax.broadcasted_iota(jnp.int32, (128, TILES * TILE), 1) // BLOCK
    block = lax.broadcasted_iota(jnp.int32, (128, TILES * TILE), 0)
    return jnp.dot(note, jnp.where(lane == block, 1.0, 0.0).astype(BF16), preferred_element_type=F32)


def square_tiles(pairs, lowest, window, notes, square):
    for k, c in pairs:
        first, last = max(k, c) - REACH, min(k, c) + REACH
        depth = slice((first - lowest) * TILE, (last + 1 - lowest) * TILE)
        total = jnp.dot(
            window[(k - lowest) * TILE : (k + 1 - lowest) * TILE, depth],
            window[depth, (c - lowest) * TILE : (c + 1 - lowest) * TILE],
            preferred_element_type=F32,
        )
        place = (c - k + REACH) * TILE
        for q in range(ROWS):
            keep = notes[k][q : q + 1, place : place + TILE] > 0.5
            square[
                pl.ds((k + REACH) * TILE + q * BLOCK, BLOCK), pl.ds((c + REACH) * TILE, TILE)
            ] = jnp.where(keep, total[q * BLOCK : (q + 1) * BLOCK], 0.0).astype(BF16)


MIDDLE = [(k, c) for k in range(-REACH, REACH + 1) for c in range(-REACH, REACH + 1) if k * c <= 0 and abs(k - c) <= REACH]
LOWER = [(k, c) for k in range(-REACH, 0) for c in range(-REACH, 0)]
UPPER = [(-k, -c) for k, c in LOWER]


def needed(pairs):
    found = set()
    for k, c in pairs:
        for l in range(max(k, c) - REACH, min(k, c) + REACH + 1):
            found.add((k, l))
            found.add((l, c))
    return sorted(found)


def middle_kernel(*refs):
    messages = dict(zip(range(-REACH, REACH + 1), refs[:TILES]))
    out_ref, window, square = refs[TILES:]
    for r, t in needed(MIDDLE):
        j = t - r + REACH
        unpack_tile(
            messages[r], j, tile_start(j, 0), window, (r + REACH) * TILE, (t + REACH) * TILE
        )
    notes = {k: spread(messages[k][DATA:, :]) for k in messages}
    square_tiles(MIDDLE, -REACH, window, notes, square)
    own = slice(REACH * TILE, (REACH + 1) * TILE)
    for c in range(-REACH, REACH + 1):
        rows = [k for k, other in MIDDLE if other == c]
        depth = slice((min(rows) + REACH) * TILE, (max(rows) + REACH + 1) * TILE)
        cols = slice((c + REACH) * TILE, (c + REACH + 1) * TILE)
        out_ref[:, cols] = jnp.dot(window[own, depth], square[depth, cols], preferred_element_type=F32)


def middle(messages):
    flops = 112 * 2 * TILE**3
    return pl.pallas_call(
        middle_kernel,
        out_shape=jax.ShapeDtypeStruct((TILE, TILES * TILE), F32),
        in_specs=[VMEM] * TILES,
        out_specs=VMEM,
        scratch_shapes=[
            pltpu.VMEM((TILES * TILE, TILES * TILE), BF16),
            pltpu.VMEM((TILES * TILE, TILES * TILE), BF16),
        ],
        compiler_params=pltpu.CompilerParams(vmem_limit_bytes=48 << 20),
        cost_estimate=pl.CostEstimate(flops=flops, bytes_accessed=8 << 20, transcendentals=0),
    )(*messages)


FAR = 2 * REACH
SPAN = 2 * FAR + 1


def corner_kernel(*refs):
    messages = dict(zip(range(-FAR, FAR + 1), refs[:SPAN]))
    part_ref, pattern_ref, out_ref, window, square = refs[SPAN:]
    for r, t in sorted(set(needed(LOWER + UPPER)) | {(0, t) for t in range(-REACH, REACH + 1)}):
        j = t - r + REACH
        first = -r if -r > REACH else 0
        unpack_tile(messages[r], j, tile_start(j, first), window, (r + FAR) * TILE, (t + FAR) * TILE)
    notes = {k: spread(messages[k][DATA:, :]) for k in range(-REACH, REACH + 1)}
    square_tiles(LOWER + UPPER, -FAR, window, notes, square)
    own = slice(FAR * TILE, (FAR + 1) * TILE)
    keep_own = notes[0]
    steps = []
    for c in range(-REACH, REACH + 1):
        cols = slice((c + REACH) * TILE, (c + REACH + 1) * TILE)
        part = part_ref[:, cols]
        if c:
            rows = (-REACH, -1) if c < 0 else (1, REACH)
            part = part + jnp.dot(
                window[own, (rows[0] + FAR) * TILE : (rows[1] + FAR + 1) * TILE],
                square[(rows[0] + REACH) * TILE : (rows[1] + REACH + 1) * TILE, cols],
                preferred_element_type=F32,
            )
        x = window[own, (c + FAR) * TILE : (c + FAR + 1) * TILE].astype(F32)
        steps.append(1.5 * x - 0.5 * part)
    width = out_ref.shape[2]
    for q in range(ROWS):
        rows = slice(q * BLOCK, (q + 1) * BLOCK)
        strip = jnp.concatenate([step[rows] for step in steps], axis=1)
        strip = jnp.where(keep_own[q : q + 1] > 0.5, strip, 0.0)
        if q % 2:
            strip = pltpu.roll(strip, TILES * TILE - BLOCK, 1)
        start = (q // 2) * 128
        out_ref[q] = strip[:, start : start + width].astype(BF16)


def corners(messages, part, pattern, out_type):
    flops = 128 * 2 * TILE**3
    return pl.pallas_call(
        corner_kernel,
        out_shape=out_type,
        in_specs=[VMEM] * (SPAN + 1) + [SMEM],
        out_specs=VMEM,
        scratch_shapes=[
            pltpu.VMEM((SPAN * TILE, SPAN * TILE), BF16),
            pltpu.VMEM((TILES * TILE, TILES * TILE), BF16),
        ],
        compiler_params=pltpu.CompilerParams(vmem_limit_bytes=56 << 20),
        cost_estimate=pl.CostEstimate(flops=flops, bytes_accessed=12 << 20, transcendentals=0),
    )(*messages, part, pattern)


def per_device(count, x, pattern):
    up = [(n, (n + 1) % count) for n in range(count)]
    down = [(n, (n - 1) % count) for n in range(count)]
    own = pack(x, pattern)
    below = own
    above = own
    held = {0: own}
    for step in range(1, REACH + 1):
        below = lax.ppermute(below, AXES, up)
        above = lax.ppermute(above, AXES, down)
        held[-step], held[step] = below, above
    part = middle([held[k] for k in range(-REACH, REACH + 1)])
    below = below[DATA - last_rows(REACH) : DATA]
    above = above[: first_rows(REACH)]
    for step in range(REACH + 1, FAR + 1):
        tiles = FAR + 1 - step
        below = lax.ppermute(below[below.shape[0] - last_rows(tiles) :], AXES, up)
        above = lax.ppermute(above[: first_rows(tiles)], AXES, down)
        if step == REACH + 1:
            below, part = lax.optimization_barrier((below, part))
        held[-step], held[step] = below, above
    return corners(
        [held[k] for k in range(-FAR, FAR + 1)], part, pattern, jax.ShapeDtypeStruct(x.shape, x.dtype)
    )


def solution(mesh):
    placed = (P(AXES, None, None), P(AXES, None))
    count = mesh.shape["row"] * mesh.shape["col"]
    return jax.shard_map(
        functools.partial(per_device, count),
        mesh=mesh,
        in_specs=placed,
        out_specs=P(AXES, None, None),
        check_vma=False,
    )
```

```python
import functools

import jax
import jax.numpy as jnp
from jax import lax
from jax.experimental import pallas as pl
from jax.experimental.pallas import tpu as pltpu
from jax.sharding import PartitionSpec as P

AXES = ("row", "col")
BLOCK = 64
ROWS = 4
TILE = ROWS * BLOCK
REACH = 3
TILES = 2 * REACH + 1
HEAD = 5 * BLOCK
BODY = 10 * TILE
TAIL = 3 * BLOCK
DATA = HEAD + BODY + TAIL
NOTE = 16
ALL = NOTE + DATA + NOTE
F32 = jnp.float32
BF16 = jnp.bfloat16
VMEM = pl.BlockSpec(memory_space=pltpu.VMEM)
SMEM = pl.BlockSpec(memory_space=pltpu.SMEM)


def first_rows(tiles):
    return HEAD + (tiles - 1) * 2 * TILE


def last_rows(tiles):
    return TAIL + (tiles - 1) * 2 * TILE


def half_lanes(rows):
    return lax.broadcasted_iota(jnp.int32, (rows, 128), 1) < BLOCK


def swap_halves(piece):
    return pltpu.roll(piece.astype(F32), BLOCK, 1)


def pack_kernel(x_ref, pattern_ref, out_ref):
    low = half_lanes(BLOCK)
    zero = jnp.zeros((BLOCK, 128), F32)
    note = jnp.zeros((NOTE, 128), F32)
    lane = lax.broadcasted_iota(jnp.int32, (NOTE, 128), 1)
    row = lax.broadcasted_iota(jnp.int32, (NOTE, 128), 0)
    slots = x_ref.shape[2] // BLOCK
    strips = []
    for q in range(ROWS):
        pieces = []
        for pair in range(slots // 2):
            even = pattern_ref[q, 2 * pair]
            odd = pattern_ref[q, 2 * pair + 1]
            keep = jnp.where(low, even, odd) == 1
            piece = x_ref[q, :, pair * 128 : (pair + 1) * 128].astype(F32)
            pieces.append(jnp.where(keep, piece, 0.0))
            for slot, present in ((2 * pair, even), (2 * pair + 1, odd)):
                value = jnp.where(present == 1, 1.0, 0.0)
                note = jnp.where((row == q) & (lane == slot + q), value, note)
        shifted = [zero] * (q // 2)
        if q % 2 == 0:
            shifted += pieces
        else:
            turned = [swap_halves(piece) for piece in pieces]
            shifted.append(jnp.where(low, 0.0, turned[0]))
            for left, right in zip(turned[:-1], turned[1:]):
                shifted.append(jnp.where(low, left, right))
            shifted.append(jnp.where(low, turned[-1], 0.0))
        shifted += [zero] * (2 * TILES - len(shifted))
        strips.append(shifted)

    def put(start, piece):
        out_ref[NOTE + start : NOTE + start + BLOCK, :] = piece.astype(BF16)

    put(0, strips[0][0])
    put(BLOCK, strips[0][1])
    put(2 * BLOCK, strips[1][1])
    put(3 * BLOCK, strips[2][1])
    put(4 * BLOCK, jnp.where(low, swap_halves(strips[3][1]), strips[1][0]))
    for pair in range(2, 2 * TILES - 2):
        for q in range(ROWS):
            put(HEAD + (pair - 2) * TILE + q * BLOCK, strips[q][pair])
    put(HEAD + BODY, strips[2][2 * TILES - 2])
    put(HEAD + BODY + BLOCK, strips[3][2 * TILES - 2])
    put(
        HEAD + BODY + 2 * BLOCK,
        jnp.where(low, strips[1][2 * TILES - 2], swap_halves(strips[3][2 * TILES - 1])),
    )
    out_ref[:NOTE, :] = note.astype(BF16)
    out_ref[NOTE + DATA :, :] = note.astype(BF16)


def pack(x, pattern):
    return pl.pallas_call(
        pack_kernel,
        out_shape=jax.ShapeDtypeStruct((ALL, 128), BF16),
        in_specs=[VMEM, SMEM],
        out_specs=VMEM,
        compiler_params=pltpu.CompilerParams(vmem_limit_bytes=32 << 20),
        cost_estimate=pl.CostEstimate(flops=1 << 20, bytes_accessed=3 << 20, transcendentals=0),
    )(x, pattern)


def unpack_tile(source, tile, base, window, row, col):
    def put(q, half, piece):
        window[pl.ds(row + q * BLOCK, BLOCK), pl.ds(col + half * 128, 128)] = piece

    low = half_lanes(BLOCK)
    zero = jnp.zeros((BLOCK, 128), BF16)
    if tile == 0:

        def seg(k):
            return source[base + k * BLOCK : base + (k + 1) * BLOCK, :]

        mixed = seg(4)
        put(0, 0, seg(0))
        put(0, 1, seg(1))
        put(1, 0, jnp.where(low, 0.0, mixed.astype(F32)).astype(BF16))
        put(1, 1, seg(2))
        put(2, 0, zero)
        put(2, 1, seg(3))
        put(3, 0, zero)
        put(3, 1, jnp.where(low, 0.0, swap_halves(mixed)).astype(BF16))
    elif tile == TILES - 1:

        def seg(k):
            return source[base + k * BLOCK : base + (k + 1) * BLOCK, :]

        mixed = seg(2)
        put(0, 0, zero)
        put(0, 1, zero)
        put(1, 0, jnp.where(low, mixed.astype(F32), 0.0).astype(BF16))
        put(1, 1, zero)
        put(2, 0, seg(0))
        put(2, 1, zero)
        put(3, 0, seg(1))
        put(3, 1, jnp.where(low, swap_halves(mixed), 0.0).astype(BF16))
    else:
        for half in range(2):
            start = base + half * TILE
            window[row : row + TILE, col + half * 128 : col + half * 128 + 128] = source[start : start + TILE, :]


def tile_start(tile, first):
    def whole(t):
        return 0 if t == 0 else HEAD + (t - 1) * 2 * TILE

    return whole(tile) - whole(first)


def spread(note):
    lane = lax.broadcasted_iota(jnp.int32, (128, TILES * TILE), 1) // BLOCK
    block = lax.broadcasted_iota(jnp.int32, (128, TILES * TILE), 0)
    return jnp.dot(note, jnp.where(lane == block, 1.0, 0.0).astype(BF16), preferred_element_type=F32)


def square_tiles(jobs, window, notes, square):
    for k, c, first, last in jobs:
        depth = slice((first + REACH) * TILE, (last + REACH + 1) * TILE)
        total = jnp.dot(
            window[(k + REACH) * TILE : (k + REACH + 1) * TILE, depth],
            window[depth, (c + REACH) * TILE : (c + REACH + 1) * TILE],
            preferred_element_type=F32,
        )
        place = (c - k + REACH) * TILE
        for q in range(ROWS):
            keep = notes[k][q : q + 1, place : place + TILE] > 0.5
            square[
                pl.ds((k + REACH) * TILE + q * BLOCK, BLOCK), pl.ds((c + REACH) * TILE, TILE)
            ] = jnp.where(keep, total[q * BLOCK : (q + 1) * BLOCK], 0.0).astype(BF16)


SPAN = range(-REACH, REACH + 1)
OWN_JOBS = [
    (k, c, max(k, c, 0) - REACH, min(k, c, 0) + REACH) for k in SPAN for c in SPAN if abs(k - c) <= REACH
]
UP_JOBS = [(k, c, max(k, c) - REACH, -1) for k in range(REACH) for c in range(REACH)]
DOWN_JOBS = [(-k, -c, 1, REACH - max(k, c)) for k in range(REACH) for c in range(REACH)]


def needed(jobs):
    return {t for k, c, first, last in jobs for l in range(first, last + 1) for t in ((k, l), (l, c))}


def load_window(refs, tiles, window):
    for r, t in sorted(tiles):
        j = t - r + REACH
        first = max(-r, 0)
        base = 0 if r < 0 else NOTE
        unpack_tile(
            refs[r + REACH],
            j,
            base + tile_start(j, first),
            window,
            (r + REACH) * TILE,
            (t + REACH) * TILE,
        )


def load_notes(refs, rows):
    return {
        k: spread(refs[k + REACH][-NOTE:, :] if k < 0 else refs[k + REACH][:NOTE, :]) for k in rows
    }


def pack_tile(total, tile, first, out_ref):
    base = tile_start(tile, first)
    low = half_lanes(BLOCK)

    def piece(q, half):
        return total[q * BLOCK : (q + 1) * BLOCK, half * 128 : half * 128 + 128]

    def put(k, value):
        out_ref[base + k * BLOCK : base + (k + 1) * BLOCK, :] = value.astype(BF16)

    if tile == 0:
        put(0, piece(0, 0))
        put(1, piece(0, 1))
        put(2, piece(1, 1))
        put(3, piece(2, 1))
        put(4, jnp.where(low, swap_halves(piece(3, 1)), piece(1, 0)))
    elif tile == TILES - 1:
        put(0, piece(2, 0))
        put(1, piece(3, 0))
        put(2, jnp.where(low, piece(1, 0), swap_halves(piece(3, 1))))
    else:
        for half in range(2):
            for q in range(ROWS):
                put(half * ROWS + q, piece(q, half))


def tile_rows(k):
    return slice((k + REACH) * TILE, (k + REACH + 1) * TILE)


def edge_kernel(*refs):
    up_ref, down_ref, window, square = refs[TILES:]
    outer = {(REACH, k) for k in range(REACH)} | {(-REACH, -k) for k in range(REACH)}
    load_window(refs, needed(UP_JOBS) | needed(DOWN_JOBS) | outer, window)
    notes = load_notes(refs, range(1 - REACH, REACH))
    for jobs, row, cols, shift, first, out_ref in (
        (UP_JOBS, REACH, range(REACH), 0, 0, up_ref),
        (DOWN_JOBS, -REACH, range(1 - REACH, 1), 2 * REACH, REACH + 1, down_ref),
    ):
        square_tiles(jobs, window, notes, square)
        depth = slice((cols[0] + REACH) * TILE, (cols[-1] + REACH + 1) * TILE)
        for c in cols:
            total = jnp.dot(
                window[tile_rows(row), depth], square[depth, tile_rows(c)], preferred_element_type=F32
            )
            pack_tile(total, c + shift, first, out_ref)


def own_kernel(*refs):
    out_ref, window, square = refs[TILES:]
    load_window(refs, needed(OWN_JOBS), window)
    square_tiles(OWN_JOBS, window, load_notes(refs, SPAN), square)
    for c in SPAN:
        depth = slice(max(c, 0) * TILE, (min(c, 0) + TILES) * TILE)
        total = jnp.dot(window[tile_rows(0), depth], square[depth, tile_rows(c)], preferred_element_type=F32)
        x = window[tile_rows(0), tile_rows(c)].astype(F32)
        out_ref[:, tile_rows(c)] = 1.5 * x - 0.5 * total


def window_call(kernel, products, out_shape, messages):
    return pl.pallas_call(
        kernel,
        out_shape=out_shape,
        in_specs=[VMEM] * TILES,
        out_specs=jax.tree.map(lambda _: VMEM, out_shape),
        scratch_shapes=[
            pltpu.VMEM((TILES * TILE, TILES * TILE), BF16),
            pltpu.VMEM((TILES * TILE, TILES * TILE), BF16),
        ],
        compiler_params=pltpu.CompilerParams(vmem_limit_bytes=48 << 20),
        cost_estimate=pl.CostEstimate(
            flops=products * 2 * TILE**3, bytes_accessed=6 << 20, transcendentals=0
        ),
    )(*messages)


def finish_kernel(part_ref, up_ref, down_ref, note_ref, out_ref, extra):
    for tile in range(REACH):
        unpack_tile(up_ref, tile, tile_start(tile, 0), extra, 0, tile * TILE)
        far = REACH + 1 + tile
        unpack_tile(down_ref, far, tile_start(far, REACH + 1), extra, 0, (REACH + tile) * TILE)
    keep = spread(note_ref[:NOTE, :])
    width = out_ref.shape[2]
    side = REACH * TILE
    for q in range(ROWS):
        rows = slice(q * BLOCK, (q + 1) * BLOCK)
        more = extra[rows, :].astype(F32)
        strip = jnp.concatenate(
            [
                part_ref[rows, :side] - 0.5 * more[:, :side],
                part_ref[rows, side : side + TILE],
                part_ref[rows, side + TILE :] - 0.5 * more[:, side:],
            ],
            axis=1,
        )
        strip = jnp.where(keep[q : q + 1] > 0.5, strip, 0.0)
        if q % 2:
            strip = pltpu.roll(strip, TILES * TILE - BLOCK, 1)
        start = (q // 2) * 128
        out_ref[q] = strip[:, start : start + width].astype(BF16)


def finish(part, up, down, own, out_type):
    return pl.pallas_call(
        finish_kernel,
        out_shape=out_type,
        in_specs=[VMEM] * 4,
        out_specs=VMEM,
        scratch_shapes=[pltpu.VMEM((TILE, 2 * REACH * TILE), BF16)],
        compiler_params=pltpu.CompilerParams(vmem_limit_bytes=32 << 20),
        cost_estimate=pl.CostEstimate(flops=4 << 20, bytes_accessed=4 << 20, transcendentals=0),
    )(part, up, down, own)


def per_device(count, x, pattern):
    def shift(steps):
        return [(n, (n + steps) % count) for n in range(count)]

    own = pack(x, pattern)
    held = {0: own}
    below = own
    above = own
    for step in range(1, REACH + 1):
        tiles = TILES - step
        below = lax.ppermute(below[below.shape[0] - NOTE - last_rows(tiles) :], AXES, shift(1))
        above = lax.ppermute(above[: NOTE + first_rows(tiles)], AXES, shift(-1))
        held[-step], held[step] = below, above
    messages = [held[k] for k in SPAN]
    up, down = window_call(
        edge_kernel,
        46,
        (
            jax.ShapeDtypeStruct((first_rows(REACH), 128), BF16),
            jax.ShapeDtypeStruct((last_rows(REACH), 128), BF16),
        ),
        messages,
    )
    part = window_call(own_kernel, 212, jax.ShapeDtypeStruct((TILE, TILES * TILE), F32), messages)
    up = lax.ppermute(up, AXES, shift(REACH))
    down = lax.ppermute(down, AXES, shift(-REACH))
    return finish(part, up, down, own, jax.ShapeDtypeStruct(x.shape, x.dtype))


def solution(mesh):
    placed = (P(AXES, None, None), P(AXES, None))
    count = mesh.shape["row"] * mesh.shape["col"]
    return jax.shard_map(
        functools.partial(per_device, count),
        mesh=mesh,
        in_specs=placed,
        out_specs=P(AXES, None, None),
        check_vma=False,
    )
```

```python
import functools

import jax
import jax.numpy as jnp
from jax import lax
from jax.experimental import pallas as pl
from jax.experimental.pallas import tpu as pltpu
from jax.sharding import PartitionSpec as P

AXES = ("row", "col")
BLOCK = 64
ROWS = 4
TILE = ROWS * BLOCK
REACH = 3
TILES = 2 * REACH + 1
HEAD = 5 * BLOCK
BODY = 10 * TILE
TAIL = 3 * BLOCK
DATA = HEAD + BODY + TAIL
NOTE = 16
ALL = NOTE + DATA + NOTE
F32 = jnp.float32
BF16 = jnp.bfloat16
VMEM = pl.BlockSpec(memory_space=pltpu.VMEM)
SMEM = pl.BlockSpec(memory_space=pltpu.SMEM)


def first_rows(tiles):
    return HEAD + (tiles - 1) * 2 * TILE


def last_rows(tiles):
    return TAIL + (tiles - 1) * 2 * TILE


SUMS = last_rows(REACH)


def half_lanes(rows):
    return lax.broadcasted_iota(jnp.int32, (rows, 128), 1) < BLOCK


def swap_halves(piece):
    return pltpu.roll(piece.astype(F32), BLOCK, 1)


def pack_kernel(x_ref, pattern_ref, out_ref):
    low = half_lanes(BLOCK)
    zero = jnp.zeros((BLOCK, 128), F32)
    note = jnp.zeros((NOTE, 128), F32)
    lane = lax.broadcasted_iota(jnp.int32, (NOTE, 128), 1)
    row = lax.broadcasted_iota(jnp.int32, (NOTE, 128), 0)
    slots = x_ref.shape[2] // BLOCK
    strips = []
    for q in range(ROWS):
        pieces = []
        for pair in range(slots // 2):
            even = pattern_ref[q, 2 * pair]
            odd = pattern_ref[q, 2 * pair + 1]
            keep = jnp.where(low, even, odd) == 1
            piece = x_ref[q, :, pair * 128 : (pair + 1) * 128].astype(F32)
            pieces.append(jnp.where(keep, piece, 0.0))
            for slot, present in ((2 * pair, even), (2 * pair + 1, odd)):
                value = jnp.where(present == 1, 1.0, 0.0)
                note = jnp.where((row == q) & (lane == slot + q), value, note)
        shifted = [zero] * (q // 2)
        if q % 2 == 0:
            shifted += pieces
        else:
            turned = [swap_halves(piece) for piece in pieces]
            shifted.append(jnp.where(low, 0.0, turned[0]))
            for left, right in zip(turned[:-1], turned[1:]):
                shifted.append(jnp.where(low, left, right))
            shifted.append(jnp.where(low, turned[-1], 0.0))
        shifted += [zero] * (2 * TILES - len(shifted))
        strips.append(shifted)

    def put(start, piece):
        out_ref[NOTE + start : NOTE + start + BLOCK, :] = piece.astype(BF16)

    put(0, strips[0][0])
    put(BLOCK, strips[0][1])
    put(2 * BLOCK, strips[1][1])
    put(3 * BLOCK, strips[2][1])
    put(4 * BLOCK, jnp.where(low, swap_halves(strips[3][1]), strips[1][0]))
    for pair in range(2, 2 * TILES - 2):
        for q in range(ROWS):
            put(HEAD + (pair - 2) * TILE + q * BLOCK, strips[q][pair])
    put(HEAD + BODY, strips[2][2 * TILES - 2])
    put(HEAD + BODY + BLOCK, strips[3][2 * TILES - 2])
    put(
        HEAD + BODY + 2 * BLOCK,
        jnp.where(low, strips[1][2 * TILES - 2], swap_halves(strips[3][2 * TILES - 1])),
    )
    out_ref[:NOTE, :] = note.astype(BF16)
    out_ref[NOTE + DATA :, :] = note.astype(BF16)


def pack(x, pattern):
    return pl.pallas_call(
        pack_kernel,
        out_shape=jax.ShapeDtypeStruct((ALL, 128), BF16),
        in_specs=[VMEM, SMEM],
        out_specs=VMEM,
        compiler_params=pltpu.CompilerParams(vmem_limit_bytes=16 << 20),
        cost_estimate=pl.CostEstimate(flops=1 << 20, bytes_accessed=3 << 20, transcendentals=0),
    )(x, pattern)


def unpack_tile(source, tile, base, window, row, col):
    def put(q, half, piece):
        window[pl.ds(row + q * BLOCK, BLOCK), pl.ds(col + half * 128, 128)] = piece

    low = half_lanes(BLOCK)
    zero = jnp.zeros((BLOCK, 128), BF16)
    if tile == 0:

        def seg(k):
            return source[base + k * BLOCK : base + (k + 1) * BLOCK, :]

        mixed = seg(4)
        put(0, 0, seg(0))
        put(0, 1, seg(1))
        put(1, 0, jnp.where(low, 0.0, mixed.astype(F32)).astype(BF16))
        put(1, 1, seg(2))
        put(2, 0, zero)
        put(2, 1, seg(3))
        put(3, 0, zero)
        put(3, 1, jnp.where(low, 0.0, swap_halves(mixed)).astype(BF16))
    elif tile == TILES - 1:

        def seg(k):
            return source[base + k * BLOCK : base + (k + 1) * BLOCK, :]

        mixed = seg(2)
        put(0, 0, zero)
        put(0, 1, zero)
        put(1, 0, jnp.where(low, mixed.astype(F32), 0.0).astype(BF16))
        put(1, 1, zero)
        put(2, 0, seg(0))
        put(2, 1, zero)
        put(3, 0, seg(1))
        put(3, 1, jnp.where(low, swap_halves(mixed), 0.0).astype(BF16))
    else:
        for half in range(2):
            start = base + half * TILE
            window[row : row + TILE, col + half * 128 : col + half * 128 + 128] = source[start : start + TILE, :]


def tile_start(tile, first):
    def whole(t):
        return 0 if t == 0 else HEAD + (t - 1) * 2 * TILE

    return whole(tile) - whole(first)


def spread(note):
    lane = lax.broadcasted_iota(jnp.int32, (128, TILES * TILE), 1) // BLOCK
    block = lax.broadcasted_iota(jnp.int32, (128, TILES * TILE), 0)
    return jnp.dot(note, jnp.where(lane == block, 1.0, 0.0).astype(BF16), preferred_element_type=F32)


def square_tiles(jobs, window, notes, square):
    for k, c, first, last in jobs:
        depth = slice((first + REACH) * TILE, (last + REACH + 1) * TILE)
        total = jnp.dot(
            window[(k + REACH) * TILE : (k + REACH + 1) * TILE, depth],
            window[depth, (c + REACH) * TILE : (c + REACH + 1) * TILE],
            preferred_element_type=F32,
        )
        place = (c - k + REACH) * TILE
        for q in range(ROWS):
            keep = notes[k][q : q + 1, place : place + TILE] > 0.5
            square[
                pl.ds((k + REACH) * TILE + q * BLOCK, BLOCK), pl.ds((c + REACH) * TILE, TILE)
            ] = jnp.where(keep, total[q * BLOCK : (q + 1) * BLOCK], 0.0).astype(BF16)


SPAN = range(-REACH, REACH + 1)
OWN_JOBS = [
    (k, c, max(k, c, 0) - REACH, min(k, c, 0) + REACH) for k in SPAN for c in SPAN if abs(k - c) <= REACH
]
UP_JOBS = [(k, c, max(k, c) - REACH, -1) for k in range(REACH) for c in range(REACH)]
DOWN_JOBS = [(-k, -c, 1, REACH - max(k, c)) for k in range(REACH) for c in range(REACH)]


def needed(jobs):
    return {t for k, c, first, last in jobs for l in range(first, last + 1) for t in ((k, l), (l, c))}


def load_window(refs, tiles, window):
    for r, t in sorted(tiles):
        j = t - r + REACH
        first = max(-r, 0)
        base = 0 if r < 0 else NOTE
        unpack_tile(
            refs[r + REACH],
            j,
            base + tile_start(j, first),
            window,
            (r + REACH) * TILE,
            (t + REACH) * TILE,
        )


def load_notes(refs, rows):
    return {
        k: spread(refs[k + REACH][-NOTE:, :] if k < 0 else refs[k + REACH][:NOTE, :]) for k in rows
    }


def pack_tile(total, tile, first, out_ref):
    base = tile_start(tile, first)
    low = half_lanes(BLOCK)

    def piece(q, half):
        return total[q * BLOCK : (q + 1) * BLOCK, half * 128 : half * 128 + 128]

    def put(k, value):
        out_ref[base + k * BLOCK : base + (k + 1) * BLOCK, :] = value.astype(BF16)

    if tile == 0:
        put(0, piece(0, 0))
        put(1, piece(0, 1))
        put(2, piece(1, 1))
        put(3, piece(2, 1))
        put(4, jnp.where(low, swap_halves(piece(3, 1)), piece(1, 0)))
    elif tile == TILES - 1:
        put(0, piece(2, 0))
        put(1, piece(3, 0))
        put(2, jnp.where(low, piece(1, 0), swap_halves(piece(3, 1))))
    else:
        for q in range(ROWS):
            put(q, piece(q, 0))
        if tile == REACH - 1:
            for q in range(2):
                put(ROWS + q, jnp.where(low, piece(q, 1), swap_halves(piece(q + 2, 1))))
        else:
            for q in range(ROWS):
                put(ROWS + q, piece(q, 1))


def tile_rows(k):
    return slice((k + REACH) * TILE, (k + REACH + 1) * TILE)


def early_kernel(*refs):
    up_ref, down_ref, near_ref, window, square = refs[TILES - 2 :]
    refs = (None,) + refs[: TILES - 2] + (None,)
    jobs = [[job for job in side if job[:2] != (0, 0)] for side in (UP_JOBS, DOWN_JOBS)]
    rest = [(0, 0, 1 - REACH, -1), (0, 0, 1, REACH - 1)]
    load_window(refs, needed(jobs[0] + jobs[1] + rest), window)
    notes = load_notes(refs, range(1 - REACH, REACH))
    for side, out_ref in enumerate((up_ref, down_ref)):
        square_tiles(jobs[side], window, notes, square)
        _, _, first, last = rest[side]
        depth = slice((first + REACH) * TILE, (last + REACH + 1) * TILE)
        near_ref[side] = jnp.dot(window[tile_rows(0), depth], window[depth, tile_rows(0)], preferred_element_type=F32)
        for k, c, _, _ in jobs[side]:
            out_ref[abs(k) * TILE : abs(k) * TILE + TILE, abs(c) * TILE : abs(c) * TILE + TILE] = square[
                tile_rows(k), tile_rows(c)
            ]


def edge_kernel(below_ref, own_ref, above_ref, up_square, down_square, near_ref, up_ref, down_ref, left, right):
    note = spread(own_ref[:NOTE, :])[:, REACH * TILE : (REACH + 1) * TILE]
    below_start = NOTE + tile_start(TILES - 1, 0)
    for side, (k, far_ref, first, base, square, out_ref) in enumerate(
        (
            (REACH, above_ref, 0, NOTE, up_square, up_ref),
            (-REACH, below_ref, REACH, 0, down_square, down_ref),
        )
    ):
        for c in range(REACH):
            j = (c if k > 0 else -c) - k + REACH
            unpack_tile(far_ref, j, base + tile_start(j, first), left, 0, c * TILE)
        if k > 0:
            unpack_tile(own_ref, 0, NOTE, left, 0, REACH * TILE)
            unpack_tile(below_ref, TILES - 1, tile_start(TILES - 1, REACH), right, 0, 0)
        else:
            unpack_tile(own_ref, TILES - 1, below_start, left, 0, REACH * TILE)
            unpack_tile(above_ref, 0, NOTE, right, 0, 0)
        near = near_ref[side] + jnp.dot(
            left[:, REACH * TILE :], right[...], preferred_element_type=F32
        )
        near = jnp.concatenate(
            [
                jnp.where(note[q : q + 1] > 0.5, near[q * BLOCK : (q + 1) * BLOCK], 0.0).astype(BF16)
                for q in range(ROWS)
            ],
            axis=0,
        )
        for c in range(REACH):
            total = jnp.dot(
                left[:, TILE : REACH * TILE],
                square[TILE:, c * TILE : (c + 1) * TILE],
                preferred_element_type=F32,
            )
            first_row = near if c == 0 else square[:TILE, c * TILE : (c + 1) * TILE]
            total = total + jnp.dot(left[:, :TILE], first_row, preferred_element_type=F32)
            if k > 0:
                pack_tile(total, c, 0, out_ref)
            else:
                pack_tile(total, 2 * REACH - c, REACH + 1, out_ref)


def own_kernel(*refs):
    out_ref, window, square = refs[TILES:]
    load_window(refs, needed(OWN_JOBS), window)
    square_tiles(OWN_JOBS, window, load_notes(refs, SPAN), square)
    for c in SPAN:
        depth = slice(max(c, 0) * TILE, (min(c, 0) + TILES) * TILE)
        total = jnp.dot(window[tile_rows(0), depth], square[depth, tile_rows(c)], preferred_element_type=F32)
        x = window[tile_rows(0), tile_rows(c)].astype(F32)
        out_ref[:, tile_rows(c)] = 1.5 * x - 0.5 * total


def call(kernel, products, out_shape, scratch, limit, operands):
    return pl.pallas_call(
        kernel,
        out_shape=out_shape,
        in_specs=[VMEM] * len(operands),
        out_specs=jax.tree.map(lambda _: VMEM, out_shape),
        scratch_shapes=[pltpu.VMEM(shape, BF16) for shape in scratch],
        compiler_params=pltpu.CompilerParams(vmem_limit_bytes=limit << 20),
        cost_estimate=pl.CostEstimate(
            flops=products * 2 * TILE**3, bytes_accessed=6 << 20, transcendentals=0
        ),
    )(*operands)


def finish_kernel(part_ref, up_ref, down_ref, note_ref, out_ref, extra):
    low = half_lanes(BLOCK)
    for tile in range(REACH):
        if tile < REACH - 1:
            unpack_tile(up_ref, tile, tile_start(tile, 0), extra, 0, tile * TILE)
        else:
            start = tile_start(tile, 0)
            cols = slice(tile * TILE + 128, tile * TILE + 256)
            extra[:, tile * TILE : tile * TILE + 128] = up_ref[start : start + TILE, :]
            for q in range(2):
                mixed = up_ref[start + TILE + q * BLOCK : start + TILE + (q + 1) * BLOCK, :]
                extra[q * BLOCK : (q + 1) * BLOCK, cols] = jnp.where(low, mixed.astype(F32), 0.0).astype(BF16)
                extra[(q + 2) * BLOCK : (q + 3) * BLOCK, cols] = jnp.where(low, swap_halves(mixed), 0.0).astype(BF16)
        far = REACH + 1 + tile
        unpack_tile(down_ref, far, tile_start(far, REACH + 1), extra, 0, (REACH + tile) * TILE)
    keep = spread(note_ref[:NOTE, :])
    width = out_ref.shape[2]
    side = REACH * TILE
    for q in range(ROWS):
        rows = slice(q * BLOCK, (q + 1) * BLOCK)
        more = extra[rows, :].astype(F32)
        strip = jnp.concatenate(
            [
                part_ref[rows, :side] - 0.5 * more[:, :side],
                part_ref[rows, side : side + TILE],
                part_ref[rows, side + TILE :] - 0.5 * more[:, side:],
            ],
            axis=1,
        )
        strip = jnp.where(keep[q : q + 1] > 0.5, strip, 0.0)
        if q % 2:
            strip = pltpu.roll(strip, TILES * TILE - BLOCK, 1)
        start = (q // 2) * 128
        out_ref[q] = strip[:, start : start + width].astype(BF16)


def finish(part, up, down, own, out_type):
    return pl.pallas_call(
        finish_kernel,
        out_shape=out_type,
        in_specs=[VMEM] * 4,
        out_specs=VMEM,
        scratch_shapes=[pltpu.VMEM((TILE, 2 * REACH * TILE), BF16)],
        compiler_params=pltpu.CompilerParams(vmem_limit_bytes=16 << 20),
        cost_estimate=pl.CostEstimate(flops=4 << 20, bytes_accessed=4 << 20, transcendentals=0),
    )(part, up, down, own)


def per_device(count, x, pattern):
    def shift(steps):
        return [(n, (n + steps) % count) for n in range(count)]

    own = pack(x, pattern)
    held = {0: own}
    below = own
    above = own
    for step in range(1, REACH + 1):
        tiles = TILES - step
        below = lax.ppermute(below[below.shape[0] - NOTE - last_rows(tiles) :], AXES, shift(1))
        above = lax.ppermute(above[: NOTE + first_rows(tiles)], AXES, shift(-1))
        held[-step], held[step] = below, above
    wide = TILES * TILE
    corner = jax.ShapeDtypeStruct((REACH * TILE, REACH * TILE), BF16)
    sums = jax.ShapeDtypeStruct((SUMS, 128), BF16)
    near = jax.ShapeDtypeStruct((2, TILE, TILE), F32)
    early = call(
        early_kernel,
        28,
        (corner, corner, near),
        [(wide, wide), (wide, wide)],
        24,
        [held[k] for k in range(1 - REACH, REACH)],
    )
    up, down = call(
        edge_kernel,
        20,
        (sums, sums),
        [(TILE, (REACH + 1) * TILE), (TILE, TILE)],
        16,
        [held[-REACH], own, held[REACH], *early],
    )
    part = call(
        own_kernel,
        212,
        jax.ShapeDtypeStruct((TILE, wide), F32),
        [(wide, wide), (wide, wide)],
        32,
        [held[k] for k in SPAN],
    )
    up = lax.ppermute(up, AXES, shift(REACH))
    down = lax.ppermute(down, AXES, shift(-REACH))
    return finish(part, up, down, own, jax.ShapeDtypeStruct(x.shape, x.dtype))


def solution(mesh):
    placed = (P(AXES, None, None), P(AXES, None))
    count = mesh.shape["row"] * mesh.shape["col"]
    return jax.shard_map(
        functools.partial(per_device, count),
        mesh=mesh,
        in_specs=placed,
        out_specs=P(AXES, None, None),
        check_vma=False,
    )
```

```python
import functools

import jax
import jax.numpy as jnp
from jax import lax
from jax.experimental import pallas as pl
from jax.experimental.pallas import tpu as pltpu
from jax.sharding import PartitionSpec as P

AXES = ("row", "col")
BLOCK = 64
ROWS = 4
TILE = ROWS * BLOCK
REACH = 3
TILES = 2 * REACH + 1
HEAD = 5 * BLOCK
BODY = 10 * TILE
TAIL = 3 * BLOCK
DATA = HEAD + BODY + TAIL
NOTE = 16
ALL = NOTE + DATA + NOTE
PAD = HEAD - TAIL
F32 = jnp.float32
BF16 = jnp.bfloat16
VMEM = pl.BlockSpec(memory_space=pltpu.VMEM)
SMEM = pl.BlockSpec(memory_space=pltpu.SMEM)


def first_rows(tiles):
    return HEAD + (tiles - 1) * 2 * TILE


def last_rows(tiles):
    return TAIL + (tiles - 1) * 2 * TILE


SUMS = last_rows(REACH)


def half_lanes(rows):
    return lax.broadcasted_iota(jnp.int32, (rows, 128), 1) < BLOCK


def swap_halves(piece):
    return pltpu.roll(piece.astype(F32), BLOCK, 1)


def pack_kernel(odd_ref, x_ref, pattern_ref, out_ref, sent_ref):
    low = half_lanes(BLOCK)
    zero = jnp.zeros((BLOCK, 128), F32)
    note = jnp.zeros((NOTE, 128), F32)
    lane = lax.broadcasted_iota(jnp.int32, (NOTE, 128), 1)
    row = lax.broadcasted_iota(jnp.int32, (NOTE, 128), 0)
    slots = x_ref.shape[2] // BLOCK
    strips = []
    for q in range(ROWS):
        pieces = []
        for pair in range(slots // 2):
            even = pattern_ref[q, 2 * pair]
            odd = pattern_ref[q, 2 * pair + 1]
            keep = jnp.where(low, even, odd) == 1
            piece = x_ref[q, :, pair * 128 : (pair + 1) * 128].astype(F32)
            pieces.append(jnp.where(keep, piece, 0.0))
            for slot, present in ((2 * pair, even), (2 * pair + 1, odd)):
                value = jnp.where(present == 1, 1.0, 0.0)
                note = jnp.where((row == q) & (lane == slot + q), value, note)
        shifted = [zero] * (q // 2)
        if q % 2 == 0:
            shifted += pieces
        else:
            turned = [swap_halves(piece) for piece in pieces]
            shifted.append(jnp.where(low, 0.0, turned[0]))
            for left, right in zip(turned[:-1], turned[1:]):
                shifted.append(jnp.where(low, left, right))
            shifted.append(jnp.where(low, turned[-1], 0.0))
        shifted += [zero] * (2 * TILES - len(shifted))
        strips.append(shifted)

    def put(start, piece):
        out_ref[NOTE + start : NOTE + start + BLOCK, :] = piece.astype(BF16)

    put(0, strips[0][0])
    put(BLOCK, strips[0][1])
    put(2 * BLOCK, strips[1][1])
    put(3 * BLOCK, strips[2][1])
    put(4 * BLOCK, jnp.where(low, swap_halves(strips[3][1]), strips[1][0]))
    for pair in range(2, 2 * TILES - 2):
        for q in range(ROWS):
            put(HEAD + (pair - 2) * TILE + q * BLOCK, strips[q][pair])
    put(HEAD + BODY, strips[2][2 * TILES - 2])
    put(HEAD + BODY + BLOCK, strips[3][2 * TILES - 2])
    put(
        HEAD + BODY + 2 * BLOCK,
        jnp.where(low, strips[1][2 * TILES - 2], swap_halves(strips[3][2 * TILES - 1])),
    )
    out_ref[:NOTE, :] = note.astype(BF16)
    out_ref[NOTE + DATA :, :] = note.astype(BF16)
    rows = sent_ref.shape[1]
    odd = odd_ref[0]
    sent_ref[odd] = out_ref[:rows, :]
    sent_ref[1 - odd] = out_ref[ALL - rows :, :]


def pack(parity, x, pattern):
    return pl.pallas_call(
        pack_kernel,
        out_shape=(
            jax.ShapeDtypeStruct((ALL, 128), BF16),
            jax.ShapeDtypeStruct((2, NOTE + first_rows(TILES - 1), 128), BF16),
        ),
        in_specs=[SMEM, VMEM, SMEM],
        out_specs=(VMEM, VMEM),
        compiler_params=pltpu.CompilerParams(vmem_limit_bytes=16 << 20),
        cost_estimate=pl.CostEstimate(flops=1 << 20, bytes_accessed=3 << 20, transcendentals=0),
    )(parity, x, pattern)


def unpack_tile(source, tile, base, window, row, col):
    def put(q, half, piece):
        window[pl.ds(row + q * BLOCK, BLOCK), pl.ds(col + half * 128, 128)] = piece

    low = half_lanes(BLOCK)
    zero = jnp.zeros((BLOCK, 128), BF16)
    if tile == 0:

        def seg(k):
            return source[base + k * BLOCK : base + (k + 1) * BLOCK, :]

        mixed = seg(4)
        put(0, 0, seg(0))
        put(0, 1, seg(1))
        put(1, 0, jnp.where(low, 0.0, mixed.astype(F32)).astype(BF16))
        put(1, 1, seg(2))
        put(2, 0, zero)
        put(2, 1, seg(3))
        put(3, 0, zero)
        put(3, 1, jnp.where(low, 0.0, swap_halves(mixed)).astype(BF16))
    elif tile == TILES - 1:

        def seg(k):
            return source[base + k * BLOCK : base + (k + 1) * BLOCK, :]

        mixed = seg(2)
        put(0, 0, zero)
        put(0, 1, zero)
        put(1, 0, jnp.where(low, mixed.astype(F32), 0.0).astype(BF16))
        put(1, 1, zero)
        put(2, 0, seg(0))
        put(2, 1, zero)
        put(3, 0, seg(1))
        put(3, 1, jnp.where(low, swap_halves(mixed), 0.0).astype(BF16))
    else:
        for half in range(2):
            start = base + half * TILE
            window[row : row + TILE, col + half * 128 : col + half * 128 + 128] = source[start : start + TILE, :]


def tile_start(tile, first):
    def whole(t):
        return 0 if t == 0 else HEAD + (t - 1) * 2 * TILE

    return whole(tile) - whole(first)


def spread(note):
    lane = lax.broadcasted_iota(jnp.int32, (128, TILES * TILE), 1) // BLOCK
    block = lax.broadcasted_iota(jnp.int32, (128, TILES * TILE), 0)
    return jnp.dot(note, jnp.where(lane == block, 1.0, 0.0).astype(BF16), preferred_element_type=F32)


def square_tiles(jobs, window, notes, square, rest=None):
    for k, c, first, last in jobs:
        depth = slice((first + REACH) * TILE, (last + REACH + 1) * TILE)
        total = jnp.dot(
            window[(k + REACH) * TILE : (k + REACH + 1) * TILE, depth],
            window[depth, (c + REACH) * TILE : (c + REACH + 1) * TILE],
            preferred_element_type=F32,
        )
        place = (c - k + REACH) * TILE
        for q in range(ROWS):
            keep = notes[k][q : q + 1, place : place + TILE] > 0.5
            value = jnp.where(keep, total[q * BLOCK : (q + 1) * BLOCK], 0.0)
            rounded = value.astype(BF16)
            at = pl.ds((k + REACH) * TILE + q * BLOCK, BLOCK), pl.ds((c + REACH) * TILE, TILE)
            square[at] = rounded
            if rest is not None and k * c > 0:
                rest[at] = (value - rounded.astype(F32)).astype(BF16)


SPAN = range(-REACH, REACH + 1)
OWN_JOBS = [
    (k, c, max(k, c, 0) - REACH, min(k, c, 0) + REACH) for k in SPAN for c in SPAN if abs(k - c) <= REACH
]
UP_JOBS = [(k, c, max(k, c) - REACH, -1) for k in range(REACH) for c in range(REACH)]
DOWN_JOBS = [(-k, -c, 1, REACH - max(k, c)) for k in range(REACH) for c in range(REACH)]


def needed(jobs):
    return {t for k, c, first, last in jobs for l in range(first, last + 1) for t in ((k, l), (l, c))}


def load_window(refs, tiles, window):
    for r, t in sorted(tiles):
        j = t - r + REACH
        first = max(-r, 0)
        base = PAD if r < 0 else NOTE
        unpack_tile(
            refs[r + REACH],
            j,
            base + tile_start(j, first),
            window,
            (r + REACH) * TILE,
            (t + REACH) * TILE,
        )


def load_notes(refs, rows):
    return {
        k: spread(refs[k + REACH][-NOTE:, :] if k < 0 else refs[k + REACH][:NOTE, :]) for k in rows
    }


def pack_tile(total, tile, first, out_ref):
    base = tile_start(tile, first)
    low = half_lanes(BLOCK)

    def piece(q, half):
        return total[q * BLOCK : (q + 1) * BLOCK, half * 128 : half * 128 + 128]

    def put(k, value):
        out_ref[base + k * BLOCK : base + (k + 1) * BLOCK, :] = value.astype(BF16)

    if tile == 0:
        put(0, piece(0, 0))
        put(1, piece(0, 1))
        put(2, piece(1, 1))
        put(3, piece(2, 1))
        put(4, jnp.where(low, swap_halves(piece(3, 1)), piece(1, 0)))
    elif tile == TILES - 1:
        put(0, piece(2, 0))
        put(1, piece(3, 0))
        put(2, jnp.where(low, piece(1, 0), swap_halves(piece(3, 1))))
    else:
        for q in range(ROWS):
            put(q, piece(q, 0))
        if tile == REACH - 1:
            for q in range(2):
                put(ROWS + q, jnp.where(low, piece(q, 1), swap_halves(piece(q + 2, 1))))
        else:
            for q in range(ROWS):
                put(ROWS + q, piece(q, 1))


def tile_rows(k):
    return slice((k + REACH) * TILE, (k + REACH + 1) * TILE)


def early_kernel(*refs):
    up_ref, down_ref, near_ref, window, square = refs[TILES - 2 :]
    refs = (None,) + refs[: TILES - 2] + (None,)
    jobs = [[job for job in side if job[:2] != (0, 0)] for side in (UP_JOBS, DOWN_JOBS)]
    rest = [(0, 0, 1 - REACH, -1), (0, 0, 1, REACH - 1)]
    load_window(refs, needed(jobs[0] + jobs[1] + rest), window)
    notes = load_notes(refs, range(1 - REACH, REACH))
    for side, out_ref in enumerate((up_ref, down_ref)):
        square_tiles(jobs[side], window, notes, square)
        _, _, first, last = rest[side]
        depth = slice((first + REACH) * TILE, (last + REACH + 1) * TILE)
        near_ref[side] = jnp.dot(window[tile_rows(0), depth], window[depth, tile_rows(0)], preferred_element_type=F32)
        for k, c, _, _ in jobs[side]:
            out_ref[abs(k) * TILE : abs(k) * TILE + TILE, abs(c) * TILE : abs(c) * TILE + TILE] = square[
                tile_rows(k), tile_rows(c)
            ]


def edge_kernel(below_ref, own_ref, above_ref, up_square, down_square, near_ref, up_ref, down_ref, left, right):
    note = spread(own_ref[:NOTE, :])[:, REACH * TILE : (REACH + 1) * TILE]
    below_start = NOTE + tile_start(TILES - 1, 0)
    for side, (k, far_ref, first, base, square, out_ref) in enumerate(
        (
            (REACH, above_ref, 0, NOTE, up_square, up_ref),
            (-REACH, below_ref, REACH, PAD, down_square, down_ref),
        )
    ):
        for c in range(REACH):
            j = (c if k > 0 else -c) - k + REACH
            unpack_tile(far_ref, j, base + tile_start(j, first), left, 0, c * TILE)
        if k > 0:
            unpack_tile(own_ref, 0, NOTE, left, 0, REACH * TILE)
            unpack_tile(below_ref, TILES - 1, PAD + tile_start(TILES - 1, REACH), right, 0, 0)
        else:
            unpack_tile(own_ref, TILES - 1, below_start, left, 0, REACH * TILE)
            unpack_tile(above_ref, 0, NOTE, right, 0, 0)
        near = near_ref[side] + jnp.dot(
            left[:, REACH * TILE :], right[...], preferred_element_type=F32
        )
        near = jnp.concatenate(
            [
                jnp.where(note[q : q + 1] > 0.5, near[q * BLOCK : (q + 1) * BLOCK], 0.0).astype(BF16)
                for q in range(ROWS)
            ],
            axis=0,
        )
        for c in range(REACH):
            total = jnp.dot(
                left[:, TILE : REACH * TILE],
                square[TILE:, c * TILE : (c + 1) * TILE],
                preferred_element_type=F32,
            )
            first_row = near if c == 0 else square[:TILE, c * TILE : (c + 1) * TILE]
            total = total + jnp.dot(left[:, :TILE], first_row, preferred_element_type=F32)
            if k > 0:
                pack_tile(total, c, 0, out_ref)
            else:
                pack_tile(total, 2 * REACH - c, REACH + 1, out_ref)


def own_kernel(*refs):
    out_ref, keep_ref, window, square, rest = refs[TILES:]
    load_window(refs, needed(OWN_JOBS), window)
    notes = load_notes(refs, SPAN)
    keep_ref[...] = notes[0]
    square_tiles(OWN_JOBS, window, notes, square, rest)
    for c in SPAN:
        depth = slice(max(c, 0) * TILE, (min(c, 0) + TILES) * TILE)
        total = jnp.dot(window[tile_rows(0), depth], square[depth, tile_rows(c)], preferred_element_type=F32)
        if c:
            depth = slice(0, REACH * TILE) if c < 0 else slice((REACH + 1) * TILE, TILES * TILE)
            total = total + jnp.dot(
                window[tile_rows(0), depth], rest[depth, tile_rows(c)], preferred_element_type=F32
            )
        x = window[tile_rows(0), tile_rows(c)].astype(F32)
        out_ref[:, tile_rows(c)] = 1.5 * x - 0.5 * total


def call(kernel, products, out_shape, scratch, limit, operands):
    return pl.pallas_call(
        kernel,
        out_shape=out_shape,
        in_specs=[VMEM] * len(operands),
        out_specs=jax.tree.map(lambda _: VMEM, out_shape),
        scratch_shapes=[pltpu.VMEM(shape, BF16) for shape in scratch],
        compiler_params=pltpu.CompilerParams(vmem_limit_bytes=limit << 20),
        cost_estimate=pl.CostEstimate(
            flops=products * 2 * TILE**3, bytes_accessed=6 << 20, transcendentals=0
        ),
    )(*operands)


def finish_kernel(part_ref, up_ref, down_ref, keep_ref, out_ref, extra):
    low = half_lanes(BLOCK)
    for tile in range(REACH):
        if tile < REACH - 1:
            unpack_tile(up_ref, tile, tile_start(tile, 0), extra, 0, tile * TILE)
        else:
            start = tile_start(tile, 0)
            cols = slice(tile * TILE + 128, tile * TILE + 256)
            extra[:, tile * TILE : tile * TILE + 128] = up_ref[start : start + TILE, :]
            for q in range(2):
                mixed = up_ref[start + TILE + q * BLOCK : start + TILE + (q + 1) * BLOCK, :]
                extra[q * BLOCK : (q + 1) * BLOCK, cols] = jnp.where(low, mixed.astype(F32), 0.0).astype(BF16)
                extra[(q + 2) * BLOCK : (q + 3) * BLOCK, cols] = jnp.where(low, swap_halves(mixed), 0.0).astype(BF16)
        far = REACH + 1 + tile
        unpack_tile(down_ref, far, tile_start(far, REACH + 1), extra, 0, (REACH + tile) * TILE)
    width = out_ref.shape[2]
    side = REACH * TILE
    for q in range(ROWS):
        rows = slice(q * BLOCK, (q + 1) * BLOCK)
        more = extra[rows, :].astype(F32)
        strip = jnp.concatenate(
            [
                part_ref[rows, :side] - 0.5 * more[:, :side],
                part_ref[rows, side : side + TILE],
                part_ref[rows, side + TILE :] - 0.5 * more[:, side:],
            ],
            axis=1,
        )
        strip = jnp.where(keep_ref[q : q + 1, :] > 0.5, strip, 0.0)
        if q % 2:
            strip = pltpu.roll(strip, TILES * TILE - BLOCK, 1)
        start = (q // 2) * 128
        out_ref[q] = strip[:, start : start + width].astype(BF16)


def finish(part, up, down, keep, out_type):
    return pl.pallas_call(
        finish_kernel,
        out_shape=out_type,
        in_specs=[VMEM] * 4,
        out_specs=VMEM,
        scratch_shapes=[pltpu.VMEM((TILE, 2 * REACH * TILE), BF16)],
        compiler_params=pltpu.CompilerParams(vmem_limit_bytes=16 << 20),
        cost_estimate=pl.CostEstimate(flops=4 << 20, bytes_accessed=4 << 20, transcendentals=0),
    )(part, up, down, keep)


def per_device(count, x, pattern):
    odd = lax.axis_index(AXES[1]) % 2
    parity = jnp.reshape(odd, (1,)).astype(jnp.int32)
    outer = [(n, (n + 1) % count if n % 2 else (n - 1) % count) for n in range(count)]
    inner = [(n, n - 1 if n % 2 else n + 1) for n in range(count)]

    def shift(steps):
        return [(n, (n + steps) % count) for n in range(count)]

    def cut(message, rows, upward):
        return lax.dynamic_slice_in_dim(message, upward * (message.shape[0] - rows), rows, 0)

    own, sent = pack(parity, x, pattern)
    held = {0: own}
    from_outer = lax.ppermute(sent[0], AXES, outer)
    from_inner = lax.ppermute(sent[1], AXES, inner)
    below = held[-1] = jnp.where(odd == 1, from_inner, from_outer)
    above = held[1] = jnp.where(odd == 1, from_outer, from_inner)
    for step in range(2, REACH + 1):
        rows = NOTE + first_rows(TILES - step)
        below, above = (
            lax.ppermute(below[below.shape[0] - rows :], AXES, shift(1)),
            lax.ppermute(above[:rows], AXES, shift(-1)),
        )
        held[-step], held[step] = below, above
    wide = TILES * TILE
    corner = jax.ShapeDtypeStruct((REACH * TILE, REACH * TILE), BF16)
    sums = jax.ShapeDtypeStruct((SUMS, 128), BF16)
    near = jax.ShapeDtypeStruct((2, TILE, TILE), F32)
    early = call(
        early_kernel,
        28,
        (corner, corner, near),
        [(wide, wide), (wide, wide)],
        24,
        [held[k] for k in range(1 - REACH, REACH)],
    )
    up, down = call(
        edge_kernel,
        20,
        (sums, sums),
        [(TILE, (REACH + 1) * TILE), (TILE, TILE)],
        16,
        [held[-REACH], own, held[REACH], *early],
    )
    part, keep = call(
        own_kernel,
        230,
        (jax.ShapeDtypeStruct((TILE, wide), F32), jax.ShapeDtypeStruct((NOTE, wide), F32)),
        [(wide, wide), (wide, wide), (wide, wide)],
        36,
        [held[k] for k in SPAN],
    )
    up = lax.ppermute(up, AXES, shift(REACH))
    down = lax.ppermute(down, AXES, shift(-REACH))
    return finish(part, up, down, keep, jax.ShapeDtypeStruct(x.shape, x.dtype))


def solution(mesh):
    placed = (P(AXES, None, None), P(AXES, None))
    count = mesh.shape["row"] * mesh.shape["col"]
    return jax.shard_map(
        functools.partial(per_device, count),
        mesh=mesh,
        in_specs=placed,
        out_specs=P(AXES, None, None),
        check_vma=False,
    )
```
